32 devices in a mesh: dp: 4 (over x, core), ev: 8 (over z, y).
Axes of the slice: x: 2, y: 2, z: 4, core: 2. Of those that a mesh axis runs over, the one named last changes fastest.
Arguments:
- events: bfloat16 [4, 1024, 512], P('dp', 'ev'), may hold values from -25 to 25
- cotangent: bfloat16 [4, 1024, 512], P('dp', 'ev'), may hold values from -6 to 6
- intra_gain: float32 [512], replicated, may hold values from 0.25 to 1.75
- intra_proj: bfloat16 [512, 1536], replicated, may hold values from -27 to 27
- intra_out: bfloat16 [512, 512], replicated, may hold values from -0.25 to 0.25
- cross_norm_gain: float32 [512], replicated, may hold values from 0.25 to 1.75
- cross_input_weight: bfloat16 [512, 1536], replicated, may hold values from -27 to 27
- cross_output_weight: bfloat16 [512, 512], replicated, may hold values from -0.25 to 0.25
- owner_map: int32 [4, 1024], P('dp'), may hold values from 0 to 7, as said below
- block_lists: int32 [4, 8, 2, 2], P('dp', 'ev'), may hold values from 0 to 1
Outputs:
- layer_out: bfloat16 [4, 1024, 512], P('dp', 'ev')
- grad_events: bfloat16 [4, 1024, 512], P('dp', 'ev')
- grad_cross_proj: float32 [512, 1536], P('ev')
- grad_cross_out: float32 [512, 512], P('ev')
The draws below stay inside these ranges and needn't reach their ends.
Inputs may be any that keep to these rules, and one draw needn't show every extreme that they name: `owner_map`: in each replica no device sends more than 32 rows to one owner.
All inputs are finite; a program needn't handle non-finite values.
Results may differ from the reference program's by a relative error of at most 0.033.
The reference program's roundings to bfloat16 on the way count: a program that leaves them out, or rounds other values in their place, can miss the bound.
Values may be sent and summed in bfloat16 or wider, within the bound.
A program may use at most 64 MiB of HBM per device.

```python
import math
import jax
import jax.numpy as jnp
from jax import lax

D = 512
HEADS = 8
HEAD_DIM = 64
EVENTS_PER_BLOCK = 128
KB = 2
ROWS_DEV = 128
REPLICAS = 4
OWNER_DEVICES = 8
ROWS = 1024
SEND_LIMIT = 32
RECEIVE_ROWS = 256
NRB = 2


def draw_events(key, part):
    base_key = jax.random.fold_in(key, 101)
    subkeys = jax.random.split(base_key, 3)
    row_scale = jnp.exp(jax.random.uniform(subkeys[0], (REPLICAS, ROWS, 1), jnp.float32, math.log(0.5), math.log(2.5)))
    col_scale = jnp.exp(jax.random.uniform(subkeys[1], (1, 1, D), jnp.float32, math.log(0.5), math.log(2.5)))
    values = jnp.clip(jax.random.normal(subkeys[2], (REPLICAS, ROWS, D), jnp.float32), -4.0, 4.0)
    return (values * row_scale * col_scale).astype(jnp.bfloat16)


def projection_draw(key):
    subkeys = jax.random.split(key, 1)
    values = jnp.clip(jax.random.normal(subkeys[0], (D, 3 * D), jnp.float32), -4.0, 4.0) * D ** (-0.5)
    return values


def draw_intra_proj(key, part):
    return projection_draw(jax.random.fold_in(key, 202)).astype(jnp.bfloat16)


def draw_cross_input_weight(key, part):
    return projection_draw(jax.random.fold_in(key, 303)).astype(jnp.bfloat16)


def draw_owner_map(key, part):
    base_key = jax.random.fold_in(key, 404)
    hot_key, order_key, slot_key = jax.random.split(base_key, 3)
    hot = jax.random.randint(hot_key, (REPLICAS, 1, 1), 0, OWNER_DEVICES)
    order_keys = jax.random.split(order_key, REPLICAS * OWNER_DEVICES)
    labels = jax.vmap(lambda subkey: jax.random.permutation(subkey, ROWS_DEV))(order_keys).reshape(REPLICAS, OWNER_DEVICES, ROWS_DEV)
    slot_keys = jax.random.split(slot_key, REPLICAS * OWNER_DEVICES)
    spread_slots = jax.vmap(lambda subkey: jax.random.permutation(subkey, (OWNER_DEVICES - 1) * SEND_LIMIT))(slot_keys).reshape(REPLICAS, OWNER_DEVICES, (OWNER_DEVICES - 1) * SEND_LIMIT)
    index = jnp.clip(labels - SEND_LIMIT, 0, (OWNER_DEVICES - 1) * SEND_LIMIT - 1)
    picked = jnp.take_along_axis(spread_slots, index, axis=2)
    others = (hot + 1 + picked // SEND_LIMIT) % OWNER_DEVICES
    targets = jnp.where(labels < SEND_LIMIT, hot, others)
    return targets.reshape(REPLICAS, ROWS).astype(jnp.int32)


def plant(entries, rng, least, high):
    longest = entries.shape.index(max(entries.shape))
    spots = []
    for shift in (0, 1):
        where = [jax.random.randint(jax.random.fold_in(rng, axis), (), 0, length) for axis, length in enumerate(entries.shape)]
        where[longest] = (where[longest] + shift) % entries.shape[longest]
        spots.append(tuple(where))
    return entries.at[spots[0]].set(least).at[spots[1]].set(high)


def shard_levels(rng, extent, cuts, smallest, high):
    factor_of, own = 1.0, jax.random.fold_in(rng, 6)
    for dim, shards_of in cuts:
        draws = jnp.exp(jax.random.uniform(jax.random.fold_in(own, dim), (shards_of,), jnp.float32, smallest / len(cuts), high / len(cuts)))
        factor_of = factor_of * jnp.repeat(draws, extent[dim] // shards_of).reshape([-1 if axis == dim else 1 for axis in range(len(extent))])
    return factor_of


def bell_draw(rng, dims, scale, most, cuts=(), held_as=jnp.bfloat16):
    loudness = shard_levels(rng, dims, cuts, -0.22, 0.18) if cuts else 1.0
    entries = jax.random.normal(rng, dims, jnp.float32) * scale * loudness
    return jnp.minimum(jnp.maximum(entries, -most), most).astype(held_as)


def setup_inputs(seed: int = 0) -> dict:
    key_list = jax.random.split(jax.random.key(seed), 11)
    return {
        "events": draw_events(jax.random.fold_in(key_list[10], 71), 0),
        "cotangent": bell_draw(key_list[1], (REPLICAS, ROWS, D), 1.0, 6.0, ((0, 4), (1, 8))),
        "intra_gain": jnp.clip(1.0 + 0.15 * jax.random.normal(key_list[2], (D,), jnp.float32), 0.25, 1.75),
        "intra_proj": draw_intra_proj(jax.random.fold_in(key_list[10], 71), 0),
        "intra_out": bell_draw(key_list[4], (D, D), D ** -0.5, 0.25),
        "cross_norm_gain": jnp.clip(1.0 + 0.15 * jax.random.normal(key_list[5], (D,), jnp.float32), 0.25, 1.75),
        "cross_input_weight": draw_cross_input_weight(jax.random.fold_in(key_list[10], 71), 0),
        "cross_output_weight": bell_draw(key_list[7], (D, D), D ** -0.5, 0.25),
        "owner_map": draw_owner_map(jax.random.fold_in(key_list[10], 71), 0),
        "block_lists": plant(jax.random.randint(key_list[9], (REPLICAS, OWNER_DEVICES, NRB, KB), 0, NRB), jax.random.fold_in(key_list[9], 1), 0, NRB - 1).astype(jnp.int32),
    }


EPSILON = 1e-05

def layer_norm(values, scale_factors):
    upcast = values.astype(jnp.float32)
    center = upcast - lax.optimization_barrier(jnp.mean(upcast, axis=-1, keepdims=True))
    spread = lax.optimization_barrier(jnp.mean(center * center, axis=-1, keepdims=True))
    return center * lax.rsqrt(spread + EPSILON) * scale_factors

def split_heads(matrix, block_groups):
    return matrix.reshape(block_groups, EVENTS_PER_BLOCK, HEADS, HEAD_DIM)

def intra_branch(source, scale_factors, input_weight, output_weight):
    row_total, features = source.shape
    block_groups = row_total // EVENTS_PER_BLOCK
    normed = layer_norm(source, scale_factors).astype(jnp.bfloat16)
    packed_rows = jnp.dot(normed, input_weight, preferred_element_type=jnp.float32).astype(jnp.bfloat16)
    queries = split_heads(packed_rows[:, :features], block_groups).astype(jnp.float32)
    key_rows = split_heads(packed_rows[:, features:2 * features], block_groups).astype(jnp.float32)
    value_rows = split_heads(packed_rows[:, 2 * features:], block_groups).astype(jnp.float32)
    scores = jnp.einsum('bqhd,bkhd->bhqk', queries, key_rows) * HEAD_DIM ** (-0.5)
    highest = lax.optimization_barrier(jnp.max(scores, axis=-1, keepdims=True))
    weights = jnp.exp(scores - highest)
    attention = (weights / lax.optimization_barrier(jnp.sum(weights, axis=-1, keepdims=True))).astype(jnp.bfloat16)
    merged_rows = jnp.einsum('bhqk,bkhd->bqhd', attention.astype(jnp.float32), value_rows)
    merged_rows = merged_rows.astype(jnp.bfloat16).reshape(row_total, features)
    branch = jnp.dot(merged_rows, output_weight, preferred_element_type=jnp.float32)
    return (source.astype(jnp.float32) + branch).astype(jnp.bfloat16)

def cross_account_inner(packed_rows, row_presence, block_listing):
    row_total, three_wide = packed_rows.shape
    features = three_wide // 3
    block_groups = row_total // EVENTS_PER_BLOCK
    selected_rows = jnp.concatenate([jnp.arange(block_groups, dtype=jnp.int32)[:, None], block_listing.astype(jnp.int32)], axis=1)
    queries = split_heads(packed_rows[:, :features].astype(jnp.float32), block_groups)
    key_rows = split_heads(packed_rows[:, features:2 * features].astype(jnp.float32), block_groups)[selected_rows]
    key_rows = key_rows.reshape(block_groups, -1, HEADS, HEAD_DIM)
    value_rows = split_heads(packed_rows[:, 2 * features:].astype(jnp.float32), block_groups)[selected_rows]
    value_rows = value_rows.reshape(block_groups, -1, HEADS, HEAD_DIM)
    key_present = row_presence.reshape(block_groups, EVENTS_PER_BLOCK)[selected_rows].reshape(block_groups, -1)
    key_total = key_present.shape[1]
    itself = jnp.arange(key_total, dtype=jnp.int32)[None, :] == jnp.arange(EVENTS_PER_BLOCK, dtype=jnp.int32)[:, None]
    allowed = key_present[:, None, None, :] | itself[None, None, :, :]
    scores = jnp.einsum('bqhd,bkhd->bhqk', queries, key_rows) * HEAD_DIM ** (-0.5)
    scores = jnp.where(allowed, scores, -1e+30)
    highest = lax.optimization_barrier(jnp.max(scores, axis=-1, keepdims=True))
    weights = jnp.where(allowed, jnp.exp(scores - highest), 0.0)
    attention = (weights / lax.optimization_barrier(jnp.sum(weights, axis=-1, keepdims=True))).astype(jnp.bfloat16)
    merged_rows = jnp.einsum('bhqk,bkhd->bqhd', attention.astype(jnp.float32), value_rows)
    return merged_rows.astype(jnp.bfloat16).reshape(row_total, features)

def owner_transfer(landed_rows, landed_cotangent, row_presence, block_listing, scale_factors, input_weight, output_weight):
    normed, norm_pull = jax.vjp(lambda input_operand: layer_norm(input_operand, scale_factors), landed_rows)
    normed_half = normed.astype(jnp.bfloat16)
    packed_rows = jnp.dot(normed_half, input_weight, preferred_element_type=jnp.float32).astype(jnp.bfloat16)
    merged_rows, central_gather = jax.vjp(lambda input_operand: cross_account_inner(input_operand, row_presence, block_listing), packed_rows)
    result = jnp.dot(merged_rows, output_weight, preferred_element_type=jnp.float32).astype(jnp.bfloat16)
    back_mixed = lax.dot_general(landed_cotangent, output_weight, (((1,), (1,)), ((), ())), preferred_element_type=jnp.float32).astype(jnp.bfloat16)
    back_packed = central_gather(back_mixed)[0]
    back_normed = lax.dot_general(back_packed, input_weight, (((1,), (1,)), ((), ())), preferred_element_type=jnp.float32)
    back_rows = norm_pull(back_normed)[0]
    return (result, back_rows, normed_half, back_packed, merged_rows)

def contract(left_part, right_part):
    return lax.dot_general(left_part, right_part, (((0,), (0,)), ((), ())), preferred_element_type=jnp.float32)

def reference(events, cotangent, intra_gain, intra_proj, intra_out, cross_norm_gain, cross_input_weight, cross_output_weight, owner_map, block_lists):

    def replica(running_total, pieces):
        rows_here, upstream, targets, block_listing = pieces
        hidden, intra_pull = jax.vjp(lambda input_operand: intra_branch(input_operand, intra_gain, intra_proj, intra_out), rows_here)
        onehot = (targets[:, None] == jnp.arange(OWNER_DEVICES, dtype=jnp.int32)[None, :]).astype(jnp.int32)
        grouped = onehot.reshape(OWNER_DEVICES, ROWS_DEV, OWNER_DEVICES)
        before = (jnp.cumsum(grouped, axis=1) - grouped).astype(jnp.int32)
        slot_ids = lax.optimization_barrier(jnp.sum(before * grouped, axis=2)).astype(jnp.int32).reshape(ROWS)
        row_counts = lax.optimization_barrier(jnp.sum(grouped, axis=1)).astype(jnp.int32)
        source = jnp.arange(ROWS, dtype=jnp.int32) // ROWS_DEV
        position = (targets * RECEIVE_ROWS + source * SEND_LIMIT + slot_ids).astype(jnp.int32)
        send_buffer = jnp.zeros((OWNER_DEVICES * RECEIVE_ROWS, D), jnp.bfloat16).at[position].set(hidden).reshape(OWNER_DEVICES, RECEIVE_ROWS, D)
        gradient_buffer = jnp.zeros((OWNER_DEVICES * RECEIVE_ROWS, D), jnp.bfloat16).at[position].set(upstream).reshape(OWNER_DEVICES, RECEIVE_ROWS, D)
        row_presence = (jnp.arange(SEND_LIMIT, dtype=jnp.int32)[None, None, :] < row_counts.T[:, :, None]).reshape(OWNER_DEVICES, RECEIVE_ROWS)

        def rows_by_owner(inner, slices):
            landed_rows, landed_cotangent, alive_rows, selected_rows = slices
            result, back_rows, normed_half, back_packed, merged_rows = owner_transfer(landed_rows, landed_cotangent, alive_rows, selected_rows, cross_norm_gain, cross_input_weight, cross_output_weight)
            partial_sum = jnp.concatenate([contract(normed_half, back_packed), contract(merged_rows, landed_cotangent)], axis=1)
            return (inner + partial_sum, (result, back_rows))
        running_total, (output_rows, returned_rows) = lax.scan(rows_by_owner, running_total, (send_buffer, gradient_buffer, row_presence, block_listing))
        result_rows = output_rows.reshape(OWNER_DEVICES * RECEIVE_ROWS, D)[position]
        layer_out = (hidden.astype(jnp.float32) + result_rows.astype(jnp.float32)).astype(jnp.bfloat16)
        return_rows = returned_rows.reshape(OWNER_DEVICES * RECEIVE_ROWS, D)[position]
        grad_hidden = (upstream.astype(jnp.float32) + return_rows.astype(jnp.float32)).astype(jnp.bfloat16)
        grad_rows = intra_pull(grad_hidden)[0]
        return (running_total, (layer_out, grad_rows))
    initial = jnp.zeros((D, 4 * D), jnp.float32)
    summed, (outputs, grads) = lax.scan(replica, initial, (events, cotangent, owner_map, block_lists))
    summed = summed * (REPLICAS * ROWS) ** (-0.5)
    return (outputs, grads, summed[:, :3 * D], summed[:, 3 * D:])
```

```python
import functools

import jax
import jax.numpy as jnp
from jax import lax
from jax.experimental import pallas as pl
from jax.experimental.pallas import tpu as pltpu
from jax.sharding import PartitionSpec as P

HEAD_DIM = 64
BLOCK = 128
SCALE = HEAD_DIM ** (-0.5)
EPSILON = 1e-05
F32 = jnp.float32
BF16 = jnp.bfloat16
VMEM_LIMIT = 50 * 1024 * 1024
MESH = pl.DeviceIdType.MESH


def dot(a, b):
    return lax.dot_general(a, b, (((1,), (0,)), ((), ())), preferred_element_type=F32)


def dot_bt(a, b):
    return lax.dot_general(a, b, (((1,), (1,)), ((), ())), preferred_element_type=F32)


def dot_at(a, b):
    return lax.dot_general(a, b, (((0,), (0,)), ((), ())), preferred_element_type=F32)


def iota(shape, dim):
    return lax.broadcasted_iota(jnp.int32, shape, dim)


def norm_stats(x):
    center = x - jnp.mean(x, axis=-1, keepdims=True)
    rstd = lax.rsqrt(jnp.mean(center * center, axis=-1, keepdims=True) + EPSILON)
    return center, rstd


def norm_back(x, gain, dy):
    center, rstd = norm_stats(x)
    xhat = center * rstd
    g = dy * gain
    return rstd * (
        g
        - jnp.mean(g, axis=-1, keepdims=True)
        - xhat * jnp.mean(g * xhat, axis=-1, keepdims=True)
    )


def lane_masks(dtype):
    lane = iota((1, 2 * HEAD_DIM), 1)
    low = jnp.where(lane < HEAD_DIM, 1.0, 0.0).astype(F32)
    return low.astype(dtype), (1.0 - low).astype(dtype)


def two_heads(x):
    low, high = lane_masks(BF16)
    return jnp.concatenate([x * low, x * high], axis=0)


def join_heads(x):
    low, high = lane_masks(F32)
    half = x.shape[0] // 2
    return x[:half] * low + x[half:] * high


def owner_rows(owner_ref, owners):
    return jnp.concatenate(
        [owner_ref[:, s * BLOCK : (s + 1) * BLOCK] for s in range(owners)], axis=0
    )


def placement(owner_ref, owners, cap, me):
    table = owner_rows(owner_ref, owners)
    own = jnp.sum(jnp.where(iota(table.shape, 0) == me, table, 0), axis=0, keepdims=True)
    onehot = jnp.where(iota((owners, BLOCK), 0) == own, 1.0, 0.0).astype(F32)
    earlier = jnp.where(iota((BLOCK, BLOCK), 0) < iota((BLOCK, BLOCK), 1), 1.0, 0.0)
    before = dot(onehot.astype(BF16), earlier.astype(BF16))
    slot = jnp.sum(before * onehot, axis=0, keepdims=True).astype(jnp.int32)
    position = own * (2 * cap) + slot
    both = jnp.concatenate([position, position + cap], axis=1)
    hit = iota((owners * 2 * cap, 2 * BLOCK), 0) == both
    return jnp.where(hit, 1.0, 0.0).astype(BF16)


def intra_forward(owners, cap, x_ref, ct_ref, gain_ref, win_ref, wout_ref, om_ref,
                  hid_ref, send_ref, packed_ref, probs_ref):
    me = lax.axis_index("ev")
    d = x_ref.shape[-1]
    x = x_ref[0].astype(F32)
    center, rstd = norm_stats(x)
    normed = (center * rstd * gain_ref[...]).astype(BF16)
    packed = dot(normed, win_ref[...]).astype(BF16)
    packed_ref[...] = packed
    mixed = []
    for t in range(d // BLOCK):
        q = packed[:, t * BLOCK : (t + 1) * BLOCK]
        k = packed[:, d + t * BLOCK : d + (t + 1) * BLOCK]
        v = packed[:, 2 * d + t * BLOCK : 2 * d + (t + 1) * BLOCK]
        s = dot_bt(two_heads(q), k) * SCALE
        w = jnp.exp(s - jnp.max(s, axis=-1, keepdims=True))
        p = w / jnp.sum(w, axis=-1, keepdims=True)
        probs_ref[t] = p
        mixed.append(join_heads(dot(p.astype(BF16), v)).astype(BF16))
    branch = dot(jnp.concatenate(mixed, axis=1), wout_ref[...])
    hidden = (x + branch).astype(BF16)
    hid_ref[...] = hidden
    place = placement(om_ref, owners, cap, me)
    stacked = jnp.concatenate([hidden, ct_ref[0]], axis=0)
    rows = dot(place, stacked).astype(BF16)
    for s in range(owners):
        send_ref[s] = rows[s * 2 * cap : (s + 1) * 2 * cap]


def greet(peers):
    barrier = pltpu.get_barrier_semaphore()
    for peer in peers:
        pl.semaphore_signal(barrier, inc=1, device_id=peer, device_id_type=MESH)
    pl.semaphore_wait(barrier, len(peers))


def exchange(owners, me, send, recv, ssem, rsem):
    copies = []
    for o in range(1, owners):
        to = lax.rem(me + o, owners)
        copies.append(
            pltpu.make_async_remote_copy(
                src_ref=send.at[to], dst_ref=recv.at[me],
                send_sem=ssem.at[o], recv_sem=rsem.at[o],
                device_id=(lax.axis_index("dp"), to), device_id_type=MESH,
            )
        )
    return copies


def exchange_kernel(owners, send_ref, out_ref, ssem, rsem):
    me = lax.axis_index("ev")
    dp = lax.axis_index("dp")
    greet([(dp, lax.rem(me + o, owners)) for o in range(1, owners)])
    copies = exchange(owners, me, send_ref, out_ref, ssem, rsem)
    for c in copies:
        c.start()
    out_ref[me] = send_ref[me]
    for c in copies:
        c.wait()


def pick(rows, columns, of_row):
    hit = iota((rows, columns), 1) == of_row(iota((rows, columns), 0))
    return jnp.where(hit, 1.0, 0.0).astype(BF16)


def cross_section(owners, cap, layout, land_ref, gain_ref, win_ref, wout_ref, om_ref, bl_ref,
                  back_ref, grad_ref):
    me = lax.axis_index("ev")
    pieces, replicas, width = layout
    total = owners * cap
    d = land_ref.shape[-1]
    if cap % 16 == 0:
        rows = jnp.concatenate([land_ref[s, 0:cap] for s in range(owners)], axis=0)
        cot = jnp.concatenate([land_ref[s, cap : 2 * cap] for s in range(owners)], axis=0)
    else:
        landed = jnp.concatenate([land_ref[s] for s in range(owners)], axis=0)
        rows = dot(pick(total, 2 * total, lambda i: i + i // cap * cap), landed).astype(BF16)
        cot = dot(pick(total, 2 * total, lambda i: i + i // cap * cap + cap), landed).astype(BF16)
    gain = gain_ref[...]
    rows32 = rows.astype(F32)
    center, rstd = norm_stats(rows32)
    normed = (center * rstd * gain).astype(BF16)
    packed = dot(normed, win_ref[...]).astype(BF16)
    back_mixed = dot_bt(cot, wout_ref[...]).astype(BF16)

    table = owner_rows(om_ref, owners)
    count = jnp.sum(jnp.where(table == me, 1, 0), axis=1, keepdims=True)
    column = iota((owners, total), 1)
    of_source = jnp.where(column // cap == iota((owners, total), 0), count, 0)
    column_count = jnp.sum(of_source, axis=0, keepdims=True)
    live = (iota((1, total), 1) % cap) < column_count
    q_row, k_row = iota((total, total), 0), iota((total, total), 1)
    times = jnp.zeros((total, total), jnp.int32)
    blocks, listed = bl_ref.shape[2], bl_ref.shape[3]
    for b in range(blocks):
        named = jnp.where(k_row // BLOCK == b, 1, 0)
        for i in range(listed):
            named = named + jnp.where(k_row // BLOCK == bl_ref[0, 0, b, i], 1, 0)
        times = jnp.where(q_row // BLOCK == b, named, times)
    times = jnp.where(live, times, jnp.where(q_row == k_row, 1, 0)).astype(F32)
    times = jnp.concatenate([times, times], axis=0)
    kept = times > 0.0

    mixed, dq, dk, dv = [], [], [], []
    for t in range(d // BLOCK):
        q = packed[:, t * BLOCK : (t + 1) * BLOCK]
        k = packed[:, d + t * BLOCK : d + (t + 1) * BLOCK]
        v = packed[:, 2 * d + t * BLOCK : 2 * d + (t + 1) * BLOCK]
        q2 = two_heads(q)
        s = jnp.where(kept, dot_bt(q2, k) * SCALE, -1e30)
        w = jnp.where(kept, jnp.exp(s - jnp.max(s, axis=-1, keepdims=True)), 0.0)
        p = w / jnp.sum(w * times, axis=-1, keepdims=True)
        pm = (p.astype(BF16).astype(F32) * times).astype(BF16)
        mixed.append(join_heads(dot(pm, v)).astype(BF16))
        dm = two_heads(back_mixed[:, t * BLOCK : (t + 1) * BLOCK])
        dp = dot_bt(dm, v).astype(BF16).astype(F32)
        pt = p * times
        ds = (pt * (dp - jnp.sum(pt * dp, axis=-1, keepdims=True)) * SCALE).astype(BF16)
        dq.append(join_heads(dot(ds, k)).astype(BF16))
        dk.append(dot_at(ds, q2).astype(BF16))
        dv.append(dot_at(pm, dm).astype(BF16))
    mixed = jnp.concatenate(mixed, axis=1)
    back_packed = jnp.concatenate(dq + dk + dv, axis=1)
    result = dot(mixed, wout_ref[...]).astype(BF16)
    back_rows = norm_back(rows32, gain, dot_bt(back_packed, win_ref[...])).astype(BF16)
    if cap % 16 == 0:
        for s in range(owners):
            back_ref[s, 0:cap] = result[s * cap : (s + 1) * cap]
            back_ref[s, cap : 2 * cap] = back_rows[s * cap : (s + 1) * cap]
    else:
        both = jnp.concatenate([result, back_rows], axis=0)
        order = pick(
            2 * total, 2 * total,
            lambda i: i // (2 * cap) * cap + i % cap + (i % (2 * cap)) // cap * total,
        )
        both = dot(order, both).astype(BF16)
        for s in range(owners):
            back_ref[s] = both[s * 2 * cap : (s + 1) * 2 * cap]
    normed_t = normed.T
    mixed_t = mixed.T
    for k in range(pieces):
        for part in range(replicas):
            at = (k * replicas + part) * width
            if at < 3 * d:
                block = dot(normed_t, back_packed[:, at : at + width])
            else:
                block = dot(mixed_t, cot[:, at - 3 * d : at - 3 * d + width])
            half = replicas // 2
            grad_ref[k, part // half, part % half] = block.astype(BF16)


def closing(owners, cap, layout, factor, back_ref, grad_ref, x_ref, ct_ref, hid_ref, packed_ref, probs_ref,
            gain_ref, win_ref, wout_ref, om_ref,
            out_ref, gx_ref, gproj_ref, gout_ref,
            ret, ra, sa, rb, sb, rc, sc, gat,
            xs, xr, as_, ar, bs, br, cs, cr, ds_, dr):
    me = lax.axis_index("ev")
    dp = lax.axis_index("dp")
    pieces, replicas, width = layout
    xs_n = replicas // 2
    x_me, core = dp // 2, dp % 2
    d = x_ref.shape[-1]
    depth = d // owners

    greet([(dp, lax.rem(me + o, owners)) for o in range(1, owners)]
          + [(lax.rem(dp + o, replicas), me) for o in range(1, replicas)])

    def remote(src, dst, ss, rs, to):
        c = pltpu.make_async_remote_copy(
            src_ref=src, dst_ref=dst, send_sem=ss, recv_sem=rs, device_id=to, device_id_type=MESH)
        c.start()
        return c

    sent = []
    rows_back = exchange(owners, me, back_ref, ret, xs, xr)
    for c in rows_back:
        c.start()
    a = [remote(grad_ref.at[k, 1 - core], ra.at[k], as_.at[k], ar.at[k], (x_me * 2 + 1 - core, me))
         for k in range(pieces)]
    b, c_, d_ = {}, {}, {}

    def after_a(k):
        a[k].wait()
        for i in range(xs_n):
            sa[k, i] = (grad_ref[k, core, i].astype(F32) + ra[k, i].astype(F32)).astype(BF16)
        b[k] = []
        for o in range(1, xs_n):
            to = lax.rem(x_me + o, xs_n)
            b[k].append(remote(sa.at[k, to], rb.at[k, o - 1], bs.at[k, o - 1], br.at[k, o - 1],
                               (to * 2 + core, me)))

    def after_b(k):
        for c in b[k]:
            c.wait()
        total = sa[k, x_me].astype(F32)
        for o in range(1, xs_n):
            total = total + rb[k, o - 1].astype(F32)
        total = total.astype(BF16)
        for e in range(owners):
            sb[k, e] = total[e * depth : (e + 1) * depth]
        c_[k] = []
        for o in range(1, owners):
            to = lax.rem(me + o, owners)
            c_[k].append(remote(sb.at[k, to], rc.at[k, o - 1], cs.at[k, o - 1], cr.at[k, o - 1], (dp, to)))

    def after_c(k):
        for c in c_[k]:
            c.wait()
        total = sb[k, me].astype(F32)
        for o in range(1, owners):
            total = total + rc[k, o - 1].astype(F32)
        total = total.astype(BF16)
        sc[k] = total
        part = core * xs_n + x_me
        gat[k, part] = total
        d_[k] = []
        for o in range(1, replicas):
            to = lax.rem(dp + o, replicas)
            d_[k].append(remote(sc.at[k], gat.at[k, part], ds_.at[k, o - 1], dr.at[k, o - 1], (to, me)))

    def after_d(k):
        for c in d_[k]:
            c.wait()
        for part in range(replicas):
            at = (k * replicas + part) * width
            value = gat[k, part].astype(F32) * factor
            if at < 3 * d:
                gproj_ref[:, at : at + width] = value
            else:
                gout_ref[:, at - 3 * d : at - 3 * d + width] = value

    ret[me] = back_ref[me]
    place = placement(om_ref, owners, cap, me)
    for k in range(pieces):
        after_a(k)
    for c in rows_back:
        c.wait()
    returned = jnp.concatenate([ret[s] for s in range(owners)], axis=0)
    rows = dot_at(place, returned)
    out_ref[0] = (hid_ref[...].astype(F32) + rows[:BLOCK]).astype(BF16)
    grad_hidden = (ct_ref[0].astype(F32) + rows[BLOCK:]).astype(BF16)
    d_mixed = dot_bt(grad_hidden, wout_ref[...]).astype(BF16)
    dq, dk, dv = [], [], []
    pairs = d // BLOCK
    for t in range(pairs):
        q = packed_ref[:, t * BLOCK : (t + 1) * BLOCK]
        k = packed_ref[:, d + t * BLOCK : d + (t + 1) * BLOCK]
        v = packed_ref[:, 2 * d + t * BLOCK : 2 * d + (t + 1) * BLOCK]
        p = probs_ref[t]
        dm = two_heads(d_mixed[:, t * BLOCK : (t + 1) * BLOCK])
        d_p = dot_bt(dm, v).astype(BF16).astype(F32)
        ds = (p * (d_p - jnp.sum(p * d_p, axis=-1, keepdims=True)) * SCALE).astype(BF16)
        dq.append(join_heads(dot(ds, k)).astype(BF16))
        dk.append(dot_at(ds, two_heads(q)).astype(BF16))
        dv.append(dot_at(p.astype(BF16), dm).astype(BF16))
    after_b(0)
    d_packed = jnp.concatenate(dq + dk + dv, axis=1)
    d_normed = dot_bt(d_packed, win_ref[...]).astype(BF16).astype(F32)
    dx = norm_back(x_ref[0].astype(F32), gain_ref[...], d_normed).astype(BF16)
    gx_ref[0] = (grad_hidden.astype(F32) + dx.astype(F32)).astype(BF16)
    for k in range(1, pieces):
        after_b(k)
    for k in range(pieces):
        after_c(k)
    for k in range(pieces):
        after_d(k)


def call(body, outs, ins, scratch=(), collective=None, smem=()):
    vm = pl.BlockSpec(memory_space=pltpu.VMEM)
    sm = pl.BlockSpec(memory_space=pltpu.SMEM)
    extra = {} if collective is None else dict(collective_id=collective, has_side_effects=True)
    return pl.pallas_call(
        body,
        out_shape=[jax.ShapeDtypeStruct(s, t) for s, t in outs],
        in_specs=[sm if i in smem else vm for i in range(len(ins))],
        out_specs=[vm] * len(outs),
        scratch_shapes=list(scratch),
        compiler_params=pltpu.CompilerParams(vmem_limit_bytes=VMEM_LIMIT, **extra),
    )(*ins)


def on_device(events, cotangent, intra_gain, intra_proj, intra_out, cross_norm_gain,
              cross_input_weight, cross_output_weight, owner_map, block_lists):
    _, local_rows, d = events.shape
    owners = lax.axis_size("ev")
    replicas = lax.axis_size("dp")
    cap = 2 * local_rows // owners
    pieces = 2
    width = 4 * d // replicas // pieces
    layout = (pieces, replicas, width)
    depth = d // owners
    half = replicas // 2
    factor = (replicas * owners * local_rows) ** (-0.5)
    gain1 = intra_gain.reshape(1, d)
    gain2 = cross_norm_gain.reshape(1, d)
    dma = pltpu.SemaphoreType.DMA
    exchanged = ((owners, 2 * cap, d), BF16)

    hidden, outgoing, packed, probs = call(
        functools.partial(intra_forward, owners, cap),
        [((local_rows, d), BF16), exchanged, ((local_rows, 3 * d), BF16),
         ((d // BLOCK, 2 * BLOCK, BLOCK), F32)],
        [events, cotangent, gain1, intra_proj, intra_out, owner_map],
    )
    [landed] = call(
        functools.partial(exchange_kernel, owners), [exchanged], [outgoing],
        [dma((owners,)), dma((owners,))], collective=0,
    )
    back, grads = call(
        functools.partial(cross_section, owners, cap, layout),
        [exchanged, ((pieces, 2, half, d, width), BF16)],
        [landed, gain2, cross_input_weight, cross_output_weight, owner_map, block_lists],
        smem=(5,),
    )
    few = max(half - 1, 1)
    scratch = [
        pltpu.VMEM((owners, 2 * cap, d), BF16),
        pltpu.VMEM((pieces, half, d, width), BF16),
        pltpu.VMEM((pieces, half, d, width), BF16),
        pltpu.VMEM((pieces, few, d, width), BF16),
        pltpu.VMEM((pieces, owners, depth, width), BF16),
        pltpu.VMEM((pieces, owners - 1, depth, width), BF16),
        pltpu.VMEM((pieces, depth, width), BF16),
        pltpu.VMEM((pieces, replicas, depth, width), BF16),
        dma((owners,)), dma((owners,)),
        dma((pieces,)), dma((pieces,)),
        dma((pieces, few)), dma((pieces, few)),
        dma((pieces, owners - 1)), dma((pieces, owners - 1)),
        dma((pieces, replicas - 1)), dma((pieces, replicas - 1)),
    ]
    return tuple(call(
        functools.partial(closing, owners, cap, layout, factor),
        [((1, local_rows, d), BF16), ((1, local_rows, d), BF16),
         ((depth, 3 * d), F32), ((depth, d), F32)],
        [back, grads, events, cotangent, hidden, packed, probs, gain1, intra_proj, intra_out, owner_map],
        scratch, collective=1,
    ))


def solution(mesh):
    row = P("dp", "ev", None)
    return jax.shard_map(
        on_device,
        mesh=mesh,
        in_specs=(row, row, P(), P(), P(), P(), P(), P(), P("dp", None), P("dp", "ev", None, None)),
        out_specs=(row, row, P("ev", None), P("ev", None)),
        check_vma=False,
    )
```

```python
import functools

import jax
import jax.numpy as jnp
from jax import lax
from jax.experimental import pallas as pl
from jax.experimental.pallas import tpu as pltpu
from jax.sharding import PartitionSpec as P

HEAD_DIM = 64
BLOCK = 128
SCALE = HEAD_DIM ** (-0.5)
EPSILON = 1e-05
F32 = jnp.float32
BF16 = jnp.bfloat16
VMEM_LIMIT = 50 * 1024 * 1024
MESH = pl.DeviceIdType.MESH


def dot(a, b):
    return lax.dot_general(a, b, (((1,), (0,)), ((), ())), preferred_element_type=F32)


def dot_bt(a, b):
    return lax.dot_general(a, b, (((1,), (1,)), ((), ())), preferred_element_type=F32)


def dot_at(a, b):
    return lax.dot_general(a, b, (((0,), (0,)), ((), ())), preferred_element_type=F32)


def iota(shape, dim):
    return lax.broadcasted_iota(jnp.int32, shape, dim)


def norm_stats(x):
    center = x - jnp.mean(x, axis=-1, keepdims=True)
    rstd = lax.rsqrt(jnp.mean(center * center, axis=-1, keepdims=True) + EPSILON)
    return center, rstd


def norm_back(x, gain, dy):
    center, rstd = norm_stats(x)
    xhat = center * rstd
    g = dy * gain
    return rstd * (
        g
        - jnp.mean(g, axis=-1, keepdims=True)
        - xhat * jnp.mean(g * xhat, axis=-1, keepdims=True)
    )


def lane_masks(dtype):
    lane = iota((1, 2 * HEAD_DIM), 1)
    low = jnp.where(lane < HEAD_DIM, 1.0, 0.0).astype(F32)
    return low.astype(dtype), (1.0 - low).astype(dtype)


def two_heads(x):
    low, high = lane_masks(BF16)
    return jnp.concatenate([x * low, x * high], axis=0)


def join_heads(x):
    low, high = lane_masks(F32)
    half = x.shape[0] // 2
    return x[:half] * low + x[half:] * high


def owner_rows(owner_ref, owners):
    return jnp.concatenate(
        [owner_ref[:, s * BLOCK : (s + 1) * BLOCK] for s in range(owners)], axis=0
    )


def placement(owner_ref, owners, cap, me):
    table = owner_rows(owner_ref, owners)
    own = jnp.sum(jnp.where(iota(table.shape, 0) == me, table, 0), axis=0, keepdims=True)
    onehot = jnp.where(iota((owners, BLOCK), 0) == own, 1.0, 0.0).astype(F32)
    earlier = jnp.where(iota((BLOCK, BLOCK), 0) < iota((BLOCK, BLOCK), 1), 1.0, 0.0)
    before = dot(onehot.astype(BF16), earlier.astype(BF16))
    slot = jnp.sum(before * onehot, axis=0, keepdims=True).astype(jnp.int32)
    hit = iota((owners * cap, BLOCK), 0) == own * cap + slot
    return jnp.where(hit, 1.0, 0.0).astype(BF16)


def split_rows(ref, rows, owners, cap):
    for s in range(owners):
        ref[s] = rows[s * cap : (s + 1) * cap].astype(BF16)


def join_rows(ref, owners, cap):
    if cap % 16 == 0:
        return jnp.concatenate([ref[s] for s in range(owners)], axis=0)
    return jnp.concatenate([ref[s].astype(F32) for s in range(owners)], axis=0).astype(BF16)


def key_counts(om_ref, bl_ref, owners, cap, me):
    total = owners * cap
    table = owner_rows(om_ref, owners)
    count = jnp.sum(jnp.where(table == me, 1, 0), axis=1, keepdims=True)
    column = iota((owners, total), 1)
    of_source = jnp.where(column // cap == iota((owners, total), 0), count, 0)
    column_count = jnp.sum(of_source, axis=0, keepdims=True)
    live = (iota((1, total), 1) % cap) < column_count
    q_row, k_row = iota((total, total), 0), iota((total, total), 1)
    times = jnp.zeros((total, total), jnp.int32)
    blocks, listed = bl_ref.shape[2], bl_ref.shape[3]
    for b in range(blocks):
        named = jnp.where(k_row // BLOCK == b, 1, 0)
        for i in range(listed):
            named = named + jnp.where(k_row // BLOCK == bl_ref[0, 0, b, i], 1, 0)
        times = jnp.where(q_row // BLOCK == b, named, times)
    times = jnp.where(live, times, jnp.where(q_row == k_row, 1, 0)).astype(F32)
    return jnp.concatenate([times, times], axis=0)


def triple(packed, t, d):
    return tuple(packed[:, i * d + t * BLOCK : i * d + (t + 1) * BLOCK] for i in range(3))


def fused(owners, cap, layout, factor,
          x_hbm, ct_hbm, om_hbm, g1_hbm, win1_hbm, wout1_hbm, g2_hbm, win2_hbm, wout2_hbm, bl_ref,
          out_ref, gx_ref, gproj_ref, gout_ref,
          x_ref, ct_ref, om_ref, g1_ref, win1_ref, wout1_ref, g2_ref, win2_ref, wout2_ref,
          packed_ref, probs_ref, hid_ref, times_ref, p2_ref, grad_ref,
          cot_s, cot_r, hid_s, hid_r, res_s, res_r, bck_s, bck_r,
          ra, sa, rb, sb, ry, sy, rc, sc, gat,
          load_sem, row_ss, row_rs, as_, ar, bs, br, ys, yr, cs, cr, ds_, dr):
    me = lax.axis_index("ev")
    dp = lax.axis_index("dp")
    pieces, replicas, width = layout
    xs_n, zs_n = replicas // 2, owners // 2
    x_me, core = dp // 2, dp % 2
    z_me, y_me = me // 2, me % 2
    d = x_ref.shape[-1]
    depth = d // owners
    pairs = d // BLOCK

    loads = {}
    for i, (name, src, dst) in enumerate([
        ("om", om_hbm, om_ref), ("ct", ct_hbm, ct_ref), ("x", x_hbm, x_ref), ("g1", g1_hbm, g1_ref),
        ("win1", win1_hbm, win1_ref), ("wout1", wout1_hbm, wout1_ref), ("g2", g2_hbm, g2_ref),
        ("win2", win2_hbm, win2_ref), ("wout2", wout2_hbm, wout2_ref),
    ]):
        loads[name] = pltpu.make_async_copy(src, dst, load_sem.at[i])
        loads[name].start()

    peers = ([(dp, lax.rem(me + o, owners)) for o in range(1, owners)]
             + [(lax.rem(dp + o, replicas), me) for o in range(1, replicas)])
    barrier = pltpu.get_barrier_semaphore()
    for peer in peers:
        pl.semaphore_signal(barrier, inc=1, device_id=peer, device_id_type=MESH)

    loads["om"].wait()
    place = placement(om_ref, owners, cap, me)
    loads["ct"].wait()
    split_rows(cot_s, dot(place, ct_ref[0]), owners, cap)
    pl.semaphore_wait(barrier, len(peers))

    def remote(src, dst, ss, rs, to):
        c = pltpu.make_async_remote_copy(
            src_ref=src, dst_ref=dst, send_sem=ss, recv_sem=rs, device_id=to, device_id_type=MESH)
        c.start()
        return c

    def exchange(n, send, recv):
        copies = []
        for o in range(1, owners):
            to = lax.rem(me + o, owners)
            copies.append(remote(send.at[to], recv.at[me], row_ss.at[n, o], row_rs.at[n, o], (dp, to)))
        recv[me] = send[me]
        return copies

    def finish(copies):
        for c in copies:
            c.wait()

    cot_x = exchange(0, cot_s, cot_r)

    for name in ("x", "g1", "win1", "wout1"):
        loads[name].wait()
    x = x_ref[0].astype(F32)
    center, rstd = norm_stats(x)
    packed = dot((center * rstd * g1_ref[...]).astype(BF16), win1_ref[...]).astype(BF16)
    packed_ref[...] = packed
    mixed = []
    for t in range(pairs):
        q, k, v = triple(packed, t, d)
        s = dot_bt(two_heads(q), k) * SCALE
        w = jnp.exp(s - jnp.max(s, axis=-1, keepdims=True))
        p = w / jnp.sum(w, axis=-1, keepdims=True)
        probs_ref[t] = p
        mixed.append(join_heads(dot(p.astype(BF16), v)).astype(BF16))
    hidden = (x + dot(jnp.concatenate(mixed, axis=1), wout1_ref[...])).astype(BF16)
    hid_ref[...] = hidden
    split_rows(hid_s, dot(place, hidden), owners, cap)
    hid_x = exchange(1, hid_s, hid_r)

    times_ref[...] = key_counts(om_ref, bl_ref, owners, cap, me)
    for name in ("g2", "win2", "wout2"):
        loads[name].wait()
    gain = g2_ref[...]
    finish(hid_x)
    rows32 = join_rows(hid_r, owners, cap).astype(F32)
    center, rstd = norm_stats(rows32)
    normed = (center * rstd * gain).astype(BF16)
    packed = dot(normed, win2_ref[...]).astype(BF16)
    mixed = []
    for t in range(pairs):
        q, k, v = triple(packed, t, d)
        times = times_ref[...]
        s = jnp.where(times > 0.0, dot_bt(two_heads(q), k) * SCALE, -1e30)
        w = jnp.where(times > 0.0, jnp.exp(s - jnp.max(s, axis=-1, keepdims=True)), 0.0)
        p = w / jnp.sum(w * times, axis=-1, keepdims=True)
        p2_ref[t] = p
        pm = (p.astype(BF16).astype(F32) * times).astype(BF16)
        mixed.append(join_heads(dot(pm, v)).astype(BF16))
    mixed = jnp.concatenate(mixed, axis=1)
    split_rows(res_s, dot(mixed, wout2_ref[...]), owners, cap)
    res_x = exchange(2, res_s, res_r)

    a, b, y_, c_, d_ = {}, {}, {}, {}, {}

    def begin(k, left_t, right):
        block = dot(left_t, right).astype(BF16)
        for part in range(replicas):
            grad_ref[k, part // xs_n, part % xs_n] = block[:, part * width : (part + 1) * width]
        a[k] = remote(grad_ref.at[k, 1 - core], ra.at[k], as_.at[k], ar.at[k],
                      (x_me * 2 + 1 - core, me))

    def after_a(k):
        a[k].wait()
        for i in range(xs_n):
            sa[k, i] = (grad_ref[k, core, i].astype(F32) + ra[k, i].astype(F32)).astype(BF16)
        b[k] = []
        for o in range(1, xs_n):
            to = lax.rem(x_me + o, xs_n)
            b[k].append(remote(sa.at[k, to], rb.at[k, o - 1], bs.at[k, o - 1], br.at[k, o - 1],
                               (to * 2 + core, me)))

    def after_b(k):
        finish(b[k])
        total = sa[k, x_me].astype(F32)
        for o in range(1, xs_n):
            total = total + rb[k, o - 1].astype(F32)
        total = total.astype(BF16)
        for e in range(owners):
            sb[k, e % 2, e // 2] = total[e * depth : (e + 1) * depth]
        y_[k] = remote(sb.at[k, 1 - y_me], ry.at[k], ys.at[k], yr.at[k], (dp, z_me * 2 + 1 - y_me))

    def after_y(k):
        y_[k].wait()
        for z in range(zs_n):
            sy[k, z] = (sb[k, y_me, z].astype(F32) + ry[k, z].astype(F32)).astype(BF16)
        c_[k] = []
        for o in range(1, zs_n):
            to = lax.rem(z_me + o, zs_n)
            c_[k].append(remote(sy.at[k, to], rc.at[k, o - 1], cs.at[k, o - 1], cr.at[k, o - 1],
                                (dp, to * 2 + y_me)))

    def after_c(k):
        finish(c_[k])
        total = sy[k, z_me].astype(F32)
        for o in range(1, zs_n):
            total = total + rc[k, o - 1].astype(F32)
        total = total.astype(BF16)
        sc[k] = total
        part = core * xs_n + x_me
        gat[k, part] = total
        d_[k] = []
        for o in range(1, replicas):
            to = lax.rem(dp + o, replicas)
            d_[k].append(remote(sc.at[k], gat.at[k, part], ds_.at[k, o - 1], dr.at[k, o - 1], (to, me)))

    def after_d(k):
        finish(d_[k])
        for part in range(replicas):
            at = (k * replicas + part) * width
            value = gat[k, part].astype(F32) * factor
            if at < 3 * d:
                gproj_ref[:, at : at + width] = value
            else:
                gout_ref[:, at - 3 * d : at - 3 * d + width] = value

    finish(cot_x)
    cot = join_rows(cot_r, owners, cap)
    span = replicas * width
    mixed_t, normed_t = mixed.T, normed.T
    early = [k for k in range(pieces) if k * span >= 3 * d]
    for k in early:
        begin(k, mixed_t, cot[:, k * span - 3 * d : (k + 1) * span - 3 * d])
    back_mixed = dot_bt(cot, wout2_ref[...]).astype(BF16)
    dq, dk, dv = [], [], []
    for t in range(pairs):
        q, k, v = triple(packed, t, d)
        p, times = p2_ref[t], times_ref[...]
        pm = (p.astype(BF16).astype(F32) * times).astype(BF16)
        dm = two_heads(back_mixed[:, t * BLOCK : (t + 1) * BLOCK])
        d_p = dot_bt(dm, v).astype(BF16).astype(F32)
        pt = p * times
        ds = (pt * (d_p - jnp.sum(pt * d_p, axis=-1, keepdims=True)) * SCALE).astype(BF16)
        dq.append(join_heads(dot(ds, k)).astype(BF16))
        dk.append(dot_at(ds, two_heads(q)).astype(BF16))
        dv.append(dot_at(pm, dm).astype(BF16))
    back_packed = jnp.concatenate(dq + dk + dv, axis=1)
    for k in range(pieces):
        if k in early:
            continue
        if (k + 1) * span <= 3 * d:
            begin(k, normed_t, back_packed[:, k * span : (k + 1) * span])
        else:
            begin_split = jnp.concatenate(
                [dot(normed_t, back_packed[:, k * span :]),
                 dot(mixed_t, cot[:, : (k + 1) * span - 3 * d])], axis=1)
            block = begin_split.astype(BF16)
            for part in range(replicas):
                grad_ref[k, part // xs_n, part % xs_n] = block[:, part * width : (part + 1) * width]
            a[k] = remote(grad_ref.at[k, 1 - core], ra.at[k], as_.at[k], ar.at[k],
                          (x_me * 2 + 1 - core, me))
    order = early + [k for k in range(pieces) if k not in early]
    for k in early:
        after_a(k)
    split_rows(bck_s, norm_back(rows32, gain, dot_bt(back_packed, win2_ref[...])), owners, cap)
    bck_x = exchange(3, bck_s, bck_r)
    for k in order:
        if k not in early:
            after_a(k)

    steps = [after_b, after_y, after_c, after_d]
    waves = [
        (step, order[w - n]) for w in range(len(order) + len(steps) - 1)
        for n, step in reversed(list(enumerate(steps))) if 0 <= w - n < len(order)]
    for step, k in waves[:3]:
        step(k)

    finish(res_x)
    finish(bck_x)
    out_ref[0] = (hid_ref[...].astype(F32) + dot_at(place, join_rows(res_r, owners, cap))).astype(BF16)
    grad_hidden = (ct_ref[0].astype(F32) + dot_at(place, join_rows(bck_r, owners, cap))).astype(BF16)
    d_mixed = dot_bt(grad_hidden, wout1_ref[...]).astype(BF16)
    dq, dk, dv = [], [], []
    for t in range(pairs):
        q, k, v = triple(packed_ref, t, d)
        p = probs_ref[t]
        dm = two_heads(d_mixed[:, t * BLOCK : (t + 1) * BLOCK])
        d_p = dot_bt(dm, v).astype(BF16).astype(F32)
        ds = (p * (d_p - jnp.sum(p * d_p, axis=-1, keepdims=True)) * SCALE).astype(BF16)
        dq.append(join_heads(dot(ds, k)).astype(BF16))
        dk.append(dot_at(ds, two_heads(q)).astype(BF16))
        dv.append(dot_at(p.astype(BF16), dm).astype(BF16))
    d_packed = jnp.concatenate(dq + dk + dv, axis=1)
    d_normed = dot_bt(d_packed, win1_ref[...]).astype(BF16).astype(F32)
    dx = norm_back(x_ref[0].astype(F32), g1_ref[...], d_normed).astype(BF16)
    gx_ref[0] = (grad_hidden.astype(F32) + dx.astype(F32)).astype(BF16)

    for step, k in waves[3:]:
        step(k)


def on_device(events, cotangent, intra_gain, intra_proj, intra_out, cross_norm_gain,
              cross_input_weight, cross_output_weight, owner_map, block_lists):
    _, local_rows, d = events.shape
    owners = lax.axis_size("ev")
    replicas = lax.axis_size("dp")
    cap = 2 * local_rows // owners
    total = owners * cap
    pieces = min(4, 4 * d // replicas // 128)
    width = 4 * d // replicas // pieces
    depth = d // owners
    half, zs = replicas // 2, owners // 2
    few = max(half - 1, 1)
    factor = (replicas * owners * local_rows) ** (-0.5)
    gain1 = intra_gain.reshape(1, d)
    gain2 = cross_norm_gain.reshape(1, d)
    dma = pltpu.SemaphoreType.DMA
    ins = [events, cotangent, owner_map, gain1, intra_proj, intra_out,
           gain2, cross_input_weight, cross_output_weight, block_lists]
    scratch = [pltpu.VMEM(a.shape, a.dtype) for a in ins[:9]] + [
        pltpu.VMEM((local_rows, 3 * d), BF16),
        pltpu.VMEM((d // BLOCK, 2 * BLOCK, BLOCK), F32),
        pltpu.VMEM((local_rows, d), BF16),
        pltpu.VMEM((2 * total, total), F32),
        pltpu.VMEM((d // BLOCK, 2 * total, total), F32),
        pltpu.VMEM((pieces, 2, half, d, width), BF16),
    ] + [pltpu.VMEM((owners, cap, d), BF16)] * 8 + [
        pltpu.VMEM((pieces, half, d, width), BF16),
        pltpu.VMEM((pieces, half, d, width), BF16),
        pltpu.VMEM((pieces, few, d, width), BF16),
        pltpu.VMEM((pieces, 2, zs, depth, width), BF16),
        pltpu.VMEM((pieces, zs, depth, width), BF16),
        pltpu.VMEM((pieces, zs, depth, width), BF16),
        pltpu.VMEM((pieces, zs - 1, depth, width), BF16),
        pltpu.VMEM((pieces, depth, width), BF16),
        pltpu.VMEM((pieces, replicas, depth, width), BF16),
        dma((9,)), dma((4, owners)), dma((4, owners)),
        dma((pieces,)), dma((pieces,)),
        dma((pieces, few)), dma((pieces, few)),
        dma((pieces,)), dma((pieces,)),
        dma((pieces, zs - 1)), dma((pieces, zs - 1)),
        dma((pieces, replicas - 1)), dma((pieces, replicas - 1)),
    ]
    vm = pl.BlockSpec(memory_space=pltpu.VMEM)
    outs = [((1, local_rows, d), BF16), ((1, local_rows, d), BF16),
            ((depth, 3 * d), F32), ((depth, d), F32)]
    return tuple(pl.pallas_call(
        functools.partial(fused, owners, cap, (pieces, replicas, width), factor),
        out_shape=[jax.ShapeDtypeStruct(s, t) for s, t in outs],
        in_specs=[pl.BlockSpec(memory_space=pltpu.HBM)] * 9 + [pl.BlockSpec(memory_space=pltpu.SMEM)],
        out_specs=[vm] * 4,
        scratch_shapes=scratch,
        compiler_params=pltpu.CompilerParams(
            vmem_limit_bytes=VMEM_LIMIT, collective_id=0, has_side_effects=True),
    )(*ins))


def solution(mesh):
    row = P("dp", "ev", None)
    return jax.shard_map(
        on_device,
        mesh=mesh,
        in_specs=(row, row, P(), P(), P(), P(), P(), P(), P("dp", None), P("dp", "ev", None, None)),
        out_specs=(row, row, P("ev", None), P("ev", None)),
        check_vma=False,
    )
```

```python
import functools

import jax
import jax.numpy as jnp
from jax import lax
from jax.experimental import pallas as pl
from jax.experimental.pallas import tpu as pltpu
from jax.sharding import PartitionSpec as P

HEAD_DIM = 64
BLOCK = 128
SCALE = HEAD_DIM ** (-0.5)
EPSILON = 1e-05
F32 = jnp.float32
BF16 = jnp.bfloat16
VMEM_LIMIT = 63 * 1024 * 1024
MESH = pl.DeviceIdType.MESH


def dot(a, b):
    return lax.dot_general(a, b, (((1,), (0,)), ((), ())), preferred_element_type=F32)


def dot_bt(a, b):
    return lax.dot_general(a, b, (((1,), (1,)), ((), ())), preferred_element_type=F32)


def dot_at(a, b):
    return lax.dot_general(a, b, (((0,), (0,)), ((), ())), preferred_element_type=F32)


def iota(shape, dim):
    return lax.broadcasted_iota(jnp.int32, shape, dim)


def norm_stats(x):
    center = x - jnp.mean(x, axis=-1, keepdims=True)
    rstd = lax.rsqrt(jnp.mean(center * center, axis=-1, keepdims=True) + EPSILON)
    return center, rstd


def norm_back(x, gain, dy):
    center, rstd = norm_stats(x)
    xhat = center * rstd
    g = dy * gain
    return rstd * (
        g
        - jnp.mean(g, axis=-1, keepdims=True)
        - xhat * jnp.mean(g * xhat, axis=-1, keepdims=True)
    )


def lane_masks(dtype):
    lane = iota((1, 2 * HEAD_DIM), 1)
    low = jnp.where(lane < HEAD_DIM, 1.0, 0.0).astype(F32)
    return low.astype(dtype), (1.0 - low).astype(dtype)


def two_heads(x):
    low, high = lane_masks(BF16)
    return jnp.concatenate([x * low, x * high], axis=0)


def join_heads(x):
    low, high = lane_masks(F32)
    half = x.shape[0] // 2
    return x[:half] * low + x[half:] * high


def owner_rows(owner_ref, owners):
    return jnp.concatenate(
        [owner_ref[:, s * BLOCK : (s + 1) * BLOCK] for s in range(owners)], axis=0
    )


def placement(owner_ref, owners, cap, me):
    table = owner_rows(owner_ref, owners)
    own = jnp.sum(jnp.where(iota(table.shape, 0) == me, table, 0), axis=0, keepdims=True)
    onehot = jnp.where(iota((owners, BLOCK), 0) == own, 1.0, 0.0).astype(F32)
    earlier = jnp.where(iota((BLOCK, BLOCK), 0) < iota((BLOCK, BLOCK), 1), 1.0, 0.0)
    before = dot(onehot.astype(BF16), earlier.astype(BF16))
    slot = jnp.sum(before * onehot, axis=0, keepdims=True).astype(jnp.int32)
    hit = iota((owners * cap, BLOCK), 0) == own * cap + slot
    return jnp.where(hit, 1.0, 0.0).astype(BF16)


def split_rows(ref, rows, owners, cap):
    for s in range(owners):
        ref[s] = rows[s * cap : (s + 1) * cap].astype(BF16)


def join_rows(ref, owners, cap):
    if cap % 16 == 0:
        return jnp.concatenate([ref[s] for s in range(owners)], axis=0)
    return jnp.concatenate([ref[s].astype(F32) for s in range(owners)], axis=0).astype(BF16)


def key_counts(om_ref, bl_ref, owners, cap, me):
    total = owners * cap
    table = owner_rows(om_ref, owners)
    count = jnp.sum(jnp.where(table == me, 1, 0), axis=1, keepdims=True)
    column = iota((owners, total), 1)
    of_source = jnp.where(column // cap == iota((owners, total), 0), count, 0)
    column_count = jnp.sum(of_source, axis=0, keepdims=True)
    live = (iota((1, total), 1) % cap) < column_count
    q_row, k_row = iota((total, total), 0), iota((total, total), 1)
    times = jnp.zeros((total, total), jnp.int32)
    blocks, listed = bl_ref.shape[2], bl_ref.shape[3]
    for b in range(blocks):
        named = jnp.where(k_row // BLOCK == b, 1, 0)
        for i in range(listed):
            named = named + jnp.where(k_row // BLOCK == bl_ref[0, 0, b, i], 1, 0)
        times = jnp.where(q_row // BLOCK == b, named, times)
    times = jnp.where(live, times, jnp.where(q_row == k_row, 1, 0)).astype(F32)
    return jnp.concatenate([times, times], axis=0)


def triple(packed, t, d):
    return tuple(packed[:, i * d + t * BLOCK : i * d + (t + 1) * BLOCK] for i in range(3))


def fused(owners, cap, layout, factor,
          x_hbm, ct_hbm, om_hbm, g1_hbm, win1_hbm, wout1_hbm, g2_hbm, win2_hbm, wout2_hbm, bl_ref,
          out_ref, gx_ref, gproj_ref, gout_ref,
          x_ref, ct_ref, om_ref, g1_ref, win1_ref, wout1_ref, g2_ref, win2_ref, wout2_ref,
          packed_ref, probs_ref, hid_ref, times_ref, p2_ref, grad_ref,
          cot_s, cot_r, hid_s, hid_r, res_s, res_r, bck_s, bck_r,
          ra, sa, rb, sb, ry, sy, rc, sc, gat,
          load_sem, row_ss, row_rs, as_, ar, bs, br, ys, yr, cs, cr, ds_, dr):
    me = lax.axis_index("ev")
    dp = lax.axis_index("dp")
    pieces, replicas, width = layout
    xs_n, zs_n = replicas // 2, owners // 2
    x_me, core = dp // 2, dp % 2
    z_me, y_me = me // 2, me % 2
    d = x_ref.shape[-1]
    depth = d // owners
    pairs = d // BLOCK

    loads = {}
    for i, (name, src, dst) in enumerate([
        ("om", om_hbm, om_ref), ("ct", ct_hbm, ct_ref), ("x", x_hbm, x_ref), ("g1", g1_hbm, g1_ref),
        ("win1", win1_hbm, win1_ref), ("wout1", wout1_hbm, wout1_ref), ("g2", g2_hbm, g2_ref),
        ("win2", win2_hbm, win2_ref), ("wout2", wout2_hbm, wout2_ref),
    ]):
        loads[name] = pltpu.make_async_copy(src, dst, load_sem.at[i])
        loads[name].start()

    peers = ([(dp, lax.rem(me + o, owners)) for o in range(1, owners)]
             + [(lax.rem(dp + o, replicas), me) for o in range(1, replicas)])
    barrier = pltpu.get_barrier_semaphore()
    for peer in peers:
        pl.semaphore_signal(barrier, inc=1, device_id=peer, device_id_type=MESH)

    loads["om"].wait()
    place = placement(om_ref, owners, cap, me)
    loads["ct"].wait()
    split_rows(cot_s, dot(place, ct_ref[0]), owners, cap)
    pl.semaphore_wait(barrier, len(peers))

    def remote(src, dst, ss, rs, to):
        c = pltpu.make_async_remote_copy(
            src_ref=src, dst_ref=dst, send_sem=ss, recv_sem=rs, device_id=to, device_id_type=MESH)
        c.start()
        return c

    def exchange(n, send, recv):
        copies = []
        for o in range(1, owners):
            to = lax.rem(me + o, owners)
            copies.append(remote(send.at[to], recv.at[me], row_ss.at[n, o], row_rs.at[n, o], (dp, to)))
        recv[me] = send[me]
        return copies

    def finish(copies):
        for c in copies:
            c.wait()

    cot_x = exchange(0, cot_s, cot_r)

    for name in ("x", "g1", "win1", "wout1"):
        loads[name].wait()
    x = x_ref[0].astype(F32)
    center, rstd = norm_stats(x)
    packed = dot((center * rstd * g1_ref[...]).astype(BF16), win1_ref[...]).astype(BF16)
    packed_ref[...] = packed
    mixed = []
    for t in range(pairs):
        q, k, v = triple(packed, t, d)
        s = dot_bt(two_heads(q), k) * SCALE
        w = jnp.exp(s - jnp.max(s, axis=-1, keepdims=True))
        p = w / jnp.sum(w, axis=-1, keepdims=True)
        probs_ref[t] = p
        mixed.append(join_heads(dot(p.astype(BF16), v)).astype(BF16))
    hidden = (x + dot(jnp.concatenate(mixed, axis=1), wout1_ref[...])).astype(BF16)
    hid_ref[...] = hidden
    split_rows(hid_s, dot(place, hidden), owners, cap)
    hid_x = exchange(1, hid_s, hid_r)

    times_ref[...] = key_counts(om_ref, bl_ref, owners, cap, me)
    for name in ("g2", "win2", "wout2"):
        loads[name].wait()
    gain = g2_ref[...]
    finish(hid_x)
    rows32 = join_rows(hid_r, owners, cap).astype(F32)
    center, rstd = norm_stats(rows32)
    normed = (center * rstd * gain).astype(BF16)
    packed = dot(normed, win2_ref[...]).astype(BF16)
    mixed = []
    for t in range(pairs):
        q, k, v = triple(packed, t, d)
        times = times_ref[...]
        s = jnp.where(times > 0.0, dot_bt(two_heads(q), k) * SCALE, -1e30)
        w = jnp.where(times > 0.0, jnp.exp(s - jnp.max(s, axis=-1, keepdims=True)), 0.0)
        p = w / jnp.sum(w * times, axis=-1, keepdims=True)
        p2_ref[t] = p
        pm = (p.astype(BF16).astype(F32) * times).astype(BF16)
        mixed.append(join_heads(dot(pm, v)).astype(BF16))
    mixed = jnp.concatenate(mixed, axis=1)
    split_rows(res_s, dot(mixed, wout2_ref[...]), owners, cap)
    res_x = exchange(2, res_s, res_r)

    a, b, y_, c_, d_ = {}, {}, {}, {}, {}

    def begin(k, left_t, right):
        block = dot(left_t, right).astype(BF16)
        for part in range(replicas):
            grad_ref[k, part // xs_n, part % xs_n] = block[:, part * width : (part + 1) * width]
        a[k] = remote(grad_ref.at[k, 1 - core], ra.at[k], as_.at[k], ar.at[k],
                      (x_me * 2 + 1 - core, me))

    def after_a(k):
        a[k].wait()
        for i in range(xs_n):
            sa[k, i] = (grad_ref[k, core, i].astype(F32) + ra[k, i].astype(F32)).astype(BF16)
        b[k] = []
        for o in range(1, xs_n):
            to = lax.rem(x_me + o, xs_n)
            b[k].append(remote(sa.at[k, to], rb.at[k, o - 1], bs.at[k, o - 1], br.at[k, o - 1],
                               (to * 2 + core, me)))

    def after_b(k):
        finish(b[k])
        total = sa[k, x_me].astype(F32)
        for o in range(1, xs_n):
            total = total + rb[k, o - 1].astype(F32)
        total = total.astype(BF16)
        for e in range(owners):
            sb[k, e % 2, e // 2] = total[e * depth : (e + 1) * depth]
        y_[k] = remote(sb.at[k, 1 - y_me], ry.at[k], ys.at[k], yr.at[k], (dp, z_me * 2 + 1 - y_me))

    def after_y(k):
        y_[k].wait()
        for z in range(zs_n):
            sy[k, z] = (sb[k, y_me, z].astype(F32) + ry[k, z].astype(F32)).astype(BF16)
        c_[k] = []
        for o in range(1, zs_n):
            to = lax.rem(z_me + o, zs_n)
            c_[k].append(remote(sy.at[k, to], rc.at[k, o - 1], cs.at[k, o - 1], cr.at[k, o - 1],
                                (dp, to * 2 + y_me)))

    def after_c(k):
        finish(c_[k])
        total = sy[k, z_me].astype(F32)
        for o in range(1, zs_n):
            total = total + rc[k, o - 1].astype(F32)
        total = total.astype(BF16)
        sc[k] = total
        part = core * xs_n + x_me
        gat[k, part] = total
        d_[k] = []
        for o in range(1, replicas):
            to = lax.rem(dp + o, replicas)
            d_[k].append(remote(sc.at[k], gat.at[k, part], ds_.at[k, o - 1], dr.at[k, o - 1], (to, me)))

    def after_d(k):
        finish(d_[k])
        for part in range(replicas):
            at = (k * replicas + part) * width
            value = gat[k, part].astype(F32) * factor
            if at < 3 * d:
                gproj_ref[:, at : at + width] = value
            else:
                gout_ref[:, at - 3 * d : at - 3 * d + width] = value

    finish(cot_x)
    cot = join_rows(cot_r, owners, cap)
    span = replicas * width
    mixed_t, normed_t = mixed.T, normed.T
    early = [k for k in range(pieces) if k * span >= 3 * d]
    for k in early:
        begin(k, mixed_t, cot[:, k * span - 3 * d : (k + 1) * span - 3 * d])
    back_mixed = dot_bt(cot, wout2_ref[...]).astype(BF16)
    dq, dk, dv = [], [], []
    for t in range(pairs):
        q, k, v = triple(packed, t, d)
        p, times = p2_ref[t], times_ref[...]
        pm = (p.astype(BF16).astype(F32) * times).astype(BF16)
        dm = two_heads(back_mixed[:, t * BLOCK : (t + 1) * BLOCK])
        d_p = dot_bt(dm, v).astype(BF16).astype(F32)
        pt = p * times
        ds = (pt * (d_p - jnp.sum(pt * d_p, axis=-1, keepdims=True)) * SCALE).astype(BF16)
        dq.append(join_heads(dot(ds, k)).astype(BF16))
        dk.append(dot_at(ds, two_heads(q)).astype(BF16))
        dv.append(dot_at(pm, dm).astype(BF16))
    back_packed = jnp.concatenate(dq + dk + dv, axis=1)
    for k in range(pieces):
        if k in early:
            continue
        if (k + 1) * span <= 3 * d:
            begin(k, normed_t, back_packed[:, k * span : (k + 1) * span])
        else:
            begin_split = jnp.concatenate(
                [dot(normed_t, back_packed[:, k * span :]),
                 dot(mixed_t, cot[:, : (k + 1) * span - 3 * d])], axis=1)
            block = begin_split.astype(BF16)
            for part in range(replicas):
                grad_ref[k, part // xs_n, part % xs_n] = block[:, part * width : (part + 1) * width]
            a[k] = remote(grad_ref.at[k, 1 - core], ra.at[k], as_.at[k], ar.at[k],
                          (x_me * 2 + 1 - core, me))
    order = early + [k for k in range(pieces) if k not in early]
    for k in early:
        after_a(k)
    split_rows(bck_s, norm_back(rows32, gain, dot_bt(back_packed, win2_ref[...])), owners, cap)
    bck_x = exchange(3, bck_s, bck_r)
    for k in order:
        if k not in early:
            after_a(k)

    steps = [after_b, after_y, after_c, after_d]
    waves = [
        (step, order[w - n]) for w in range(len(order) + len(steps) - 1)
        for n, step in reversed(list(enumerate(steps))) if 0 <= w - n < len(order)]
    for step, k in waves[:3]:
        step(k)

    finish(res_x)
    finish(bck_x)
    out_ref[0] = (hid_ref[...].astype(F32) + dot_at(place, join_rows(res_r, owners, cap))).astype(BF16)
    grad_hidden = (ct_ref[0].astype(F32) + dot_at(place, join_rows(bck_r, owners, cap))).astype(BF16)
    d_mixed = dot_bt(grad_hidden, wout1_ref[...]).astype(BF16)
    dq, dk, dv = [], [], []
    for t in range(pairs):
        q, k, v = triple(packed_ref, t, d)
        p = probs_ref[t]
        dm = two_heads(d_mixed[:, t * BLOCK : (t + 1) * BLOCK])
        d_p = dot_bt(dm, v).astype(BF16).astype(F32)
        ds = (p * (d_p - jnp.sum(p * d_p, axis=-1, keepdims=True)) * SCALE).astype(BF16)
        dq.append(join_heads(dot(ds, k)).astype(BF16))
        dk.append(dot_at(ds, two_heads(q)).astype(BF16))
        dv.append(dot_at(p.astype(BF16), dm).astype(BF16))
    d_packed = jnp.concatenate(dq + dk + dv, axis=1)
    d_normed = dot_bt(d_packed, win1_ref[...]).astype(BF16).astype(F32)
    dx = norm_back(x_ref[0].astype(F32), g1_ref[...], d_normed).astype(BF16)
    gx_ref[0] = (grad_hidden.astype(F32) + dx.astype(F32)).astype(BF16)

    for step, k in waves[3:]:
        step(k)


def on_device(events, cotangent, intra_gain, intra_proj, intra_out, cross_norm_gain,
              cross_input_weight, cross_output_weight, owner_map, block_lists):
    _, local_rows, d = events.shape
    owners = lax.axis_size("ev")
    replicas = lax.axis_size("dp")
    cap = 2 * local_rows // owners
    total = owners * cap
    pieces = min(4, 4 * d // replicas // 128)
    width = 4 * d // replicas // pieces
    depth = d // owners
    half, zs = replicas // 2, owners // 2
    few = max(half - 1, 1)
    factor = (replicas * owners * local_rows) ** (-0.5)
    gain1 = intra_gain.reshape(1, d)
    gain2 = cross_norm_gain.reshape(1, d)
    dma = pltpu.SemaphoreType.DMA
    ins = [events, cotangent, owner_map, gain1, intra_proj, intra_out,
           gain2, cross_input_weight, cross_output_weight, block_lists]
    scratch = [pltpu.VMEM(a.shape, a.dtype) for a in ins[:9]] + [
        pltpu.VMEM((local_rows, 3 * d), BF16),
        pltpu.VMEM((d // BLOCK, 2 * BLOCK, BLOCK), F32),
        pltpu.VMEM((local_rows, d), BF16),
        pltpu.VMEM((2 * total, total), F32),
        pltpu.VMEM((d // BLOCK, 2 * total, total), F32),
        pltpu.VMEM((pieces, 2, half, d, width), BF16),
    ] + [pltpu.VMEM((owners, cap, d), BF16)] * 8 + [
        pltpu.VMEM((pieces, half, d, width), BF16),
        pltpu.VMEM((pieces, half, d, width), BF16),
        pltpu.VMEM((pieces, few, d, width), BF16),
        pltpu.VMEM((pieces, 2, zs, depth, width), BF16),
        pltpu.VMEM((pieces, zs, depth, width), BF16),
        pltpu.VMEM((pieces, zs, depth, width), BF16),
        pltpu.VMEM((pieces, zs - 1, depth, width), BF16),
        pltpu.VMEM((pieces, depth, width), BF16),
        pltpu.VMEM((pieces, replicas, depth, width), BF16),
        dma((9,)), dma((4, owners)), dma((4, owners)),
        dma((pieces,)), dma((pieces,)),
        dma((pieces, few)), dma((pieces, few)),
        dma((pieces,)), dma((pieces,)),
        dma((pieces, zs - 1)), dma((pieces, zs - 1)),
        dma((pieces, replicas - 1)), dma((pieces, replicas - 1)),
    ]
    vm = pl.BlockSpec(memory_space=pltpu.VMEM)
    outs = [((1, local_rows, d), BF16), ((1, local_rows, d), BF16),
            ((depth, 3 * d), F32), ((depth, d), F32)]
    return tuple(pl.pallas_call(
        functools.partial(fused, owners, cap, (pieces, replicas, width), factor),
        out_shape=[jax.ShapeDtypeStruct(s, t) for s, t in outs],
        in_specs=[pl.BlockSpec(memory_space=pltpu.HBM)] * 9 + [pl.BlockSpec(memory_space=pltpu.SMEM)],
        out_specs=[vm] * 4,
        scratch_shapes=scratch,
        compiler_params=pltpu.CompilerParams(
            vmem_limit_bytes=VMEM_LIMIT, collective_id=0, has_side_effects=True),
    )(*ins))


def solution(mesh):
    row = P("dp", "ev", None)
    return jax.shard_map(
        on_device,
        mesh=mesh,
        in_specs=(row, row, P(), P(), P(), P(), P(), P(), P("dp", None), P("dp", "ev", None, None)),
        out_specs=(row, row, P("ev", None), P("ev", None)),
        check_vma=False,
    )
```

```python
import functools

import jax
import jax.numpy as jnp
from jax import lax
from jax.experimental import pallas as pl
from jax.experimental.pallas import tpu as pltpu
from jax.sharding import PartitionSpec as P

HEAD_DIM = 64
BLOCK = 128
SCALE = HEAD_DIM ** (-0.5)
EPSILON = 1e-05
F32 = jnp.float32
BF16 = jnp.bfloat16
VMEM_LIMIT = 63 * 1024 * 1024
MESH = pl.DeviceIdType.MESH


def dot(a, b):
    return lax.dot_general(a, b, (((1,), (0,)), ((), ())), preferred_element_type=F32)


def dot_bt(a, b):
    return lax.dot_general(a, b, (((1,), (1,)), ((), ())), preferred_element_type=F32)


def dot_at(a, b):
    return lax.dot_general(a, b, (((0,), (0,)), ((), ())), preferred_element_type=F32)


def iota(shape, dim):
    return lax.broadcasted_iota(jnp.int32, shape, dim)


def norm_stats(x):
    center = x - jnp.mean(x, axis=-1, keepdims=True)
    rstd = lax.rsqrt(jnp.mean(center * center, axis=-1, keepdims=True) + EPSILON)
    return center, rstd


def norm_back(x, gain, dy):
    center, rstd = norm_stats(x)
    xhat = center * rstd
    g = dy * gain
    return rstd * (
        g
        - jnp.mean(g, axis=-1, keepdims=True)
        - xhat * jnp.mean(g * xhat, axis=-1, keepdims=True)
    )


def lane_masks(dtype):
    lane = iota((1, 2 * HEAD_DIM), 1)
    low = jnp.where(lane < HEAD_DIM, 1.0, 0.0).astype(F32)
    return low.astype(dtype), (1.0 - low).astype(dtype)


def two_heads(x):
    low, high = lane_masks(BF16)
    return jnp.concatenate([x * low, x * high], axis=0)


def join_heads(x):
    low, high = lane_masks(F32)
    half = x.shape[0] // 2
    return x[:half] * low + x[half:] * high


def owner_rows(owner_ref, owners):
    return jnp.concatenate(
        [owner_ref[:, s * BLOCK : (s + 1) * BLOCK] for s in range(owners)], axis=0
    )


def placement(owner_ref, owners, cap, me):
    table = owner_rows(owner_ref, owners)
    own = jnp.sum(jnp.where(iota(table.shape, 0) == me, table, 0), axis=0, keepdims=True)
    onehot = jnp.where(iota((owners, BLOCK), 0) == own, 1.0, 0.0).astype(F32)
    earlier = jnp.where(iota((BLOCK, BLOCK), 0) < iota((BLOCK, BLOCK), 1), 1.0, 0.0)
    before = dot(onehot.astype(BF16), earlier.astype(BF16))
    slot = jnp.sum(before * onehot, axis=0, keepdims=True).astype(jnp.int32)
    hit = iota((owners * cap, BLOCK), 0) == own * cap + slot
    return jnp.where(hit, 1.0, 0.0).astype(BF16)


def split_rows(ref, rows, owners, cap):
    for s in range(owners):
        ref[s] = rows[s * cap : (s + 1) * cap].astype(BF16)


def join_rows(ref, owners, cap):
    if cap % 16 == 0:
        return jnp.concatenate([ref[s] for s in range(owners)], axis=0)
    return jnp.concatenate([ref[s].astype(F32) for s in range(owners)], axis=0).astype(BF16)


def key_counts(om_ref, bl_ref, owners, cap, me):
    total = owners * cap
    table = owner_rows(om_ref, owners)
    count = jnp.sum(jnp.where(table == me, 1, 0), axis=1, keepdims=True)
    column = iota((owners, total), 1)
    of_source = jnp.where(column // cap == iota((owners, total), 0), count, 0)
    column_count = jnp.sum(of_source, axis=0, keepdims=True)
    live = (iota((1, total), 1) % cap) < column_count
    q_row, k_row = iota((total, total), 0), iota((total, total), 1)
    times = jnp.zeros((total, total), jnp.int32)
    blocks, listed = bl_ref.shape[2], bl_ref.shape[3]
    for b in range(blocks):
        named = jnp.where(k_row // BLOCK == b, 1, 0)
        for i in range(listed):
            named = named + jnp.where(k_row // BLOCK == bl_ref[0, 0, b, i], 1, 0)
        times = jnp.where(q_row // BLOCK == b, named, times)
    times = jnp.where(live, times, jnp.where(q_row == k_row, 1, 0)).astype(F32)
    return jnp.concatenate([times, times], axis=0)


def triple(packed, t, d):
    return tuple(packed[:, i * d + t * BLOCK : i * d + (t + 1) * BLOCK] for i in range(3))


def fused(owners, cap, layout, factor,
          x_hbm, ct_hbm, om_hbm, g1_hbm, win1_hbm, wout1_hbm, g2_hbm, win2_hbm, wout2_hbm, bl_ref,
          out_ref, gx_ref, gproj_ref, gout_ref,
          x_ref, ct_ref, om_ref, g1_ref, win1_ref, wout1_ref, g2_ref, win2_ref, wout2_ref,
          packed_ref, probs_ref, hid_ref, times_ref, p2_ref, grad_ref,
          cot_s, cot_r, hid_s, hid_r, res_s, res_r, bck_s, bck_r,
          ra, sa, rb, sb, ry, sy, rc, sc, gat,
          load_sem, row_ss, row_rs, as_, ar, bs, br, ys, yr, cs, cr, ds_, dr):
    me = lax.axis_index("ev")
    dp = lax.axis_index("dp")
    pieces, replicas, width = layout
    xs_n, zs_n = replicas // 2, owners // 2
    x_me, core = dp // 2, dp % 2
    z_me, y_me = me // 2, me % 2
    d = x_ref.shape[-1]
    depth = d // owners
    pairs = d // BLOCK

    loads = {}
    for i, (name, src, dst) in enumerate([
        ("om", om_hbm, om_ref), ("ct", ct_hbm, ct_ref), ("x", x_hbm, x_ref), ("g1", g1_hbm, g1_ref),
        ("win1", win1_hbm, win1_ref), ("wout1", wout1_hbm, wout1_ref), ("g2", g2_hbm, g2_ref),
        ("win2", win2_hbm, win2_ref), ("wout2", wout2_hbm, wout2_ref),
    ]):
        loads[name] = pltpu.make_async_copy(src, dst, load_sem.at[i])
        loads[name].start()

    peers = ([(dp, lax.rem(me + o, owners)) for o in range(1, owners)]
             + [(lax.rem(dp + o, replicas), me) for o in range(1, replicas)])
    barrier = pltpu.get_barrier_semaphore()
    for peer in peers:
        pl.semaphore_signal(barrier, inc=1, device_id=peer, device_id_type=MESH)

    loads["om"].wait()
    place = placement(om_ref, owners, cap, me)
    loads["ct"].wait()
    split_rows(cot_s, dot(place, ct_ref[0]), owners, cap)
    pl.semaphore_wait(barrier, len(peers))

    def remote(src, dst, ss, rs, to):
        c = pltpu.make_async_remote_copy(
            src_ref=src, dst_ref=dst, send_sem=ss, recv_sem=rs, device_id=to, device_id_type=MESH)
        c.start()
        return c

    def exchange(n, send, recv):
        copies = []
        for o in range(1, owners):
            to = lax.rem(me + o, owners)
            copies.append(remote(send.at[to], recv.at[me], row_ss.at[n, o], row_rs.at[n, o], (dp, to)))
        recv[me] = send[me]
        return copies

    def finish(copies):
        for c in copies:
            c.wait()

    cot_x = exchange(0, cot_s, cot_r)

    for name in ("x", "g1", "win1", "wout1"):
        loads[name].wait()
    x = x_ref[0].astype(F32)
    center, rstd = norm_stats(x)
    packed = dot((center * rstd * g1_ref[...]).astype(BF16), win1_ref[...]).astype(BF16)
    packed_ref[...] = packed
    mixed = []
    for t in range(pairs):
        q, k, v = triple(packed, t, d)
        s = dot_bt(two_heads(q), k) * SCALE
        w = jnp.exp(s - jnp.max(s, axis=-1, keepdims=True))
        p = w / jnp.sum(w, axis=-1, keepdims=True)
        probs_ref[t] = p
        mixed.append(join_heads(dot(p.astype(BF16), v)).astype(BF16))
    hidden = (x + dot(jnp.concatenate(mixed, axis=1), wout1_ref[...])).astype(BF16)
    hid_ref[...] = hidden
    split_rows(hid_s, dot(place, hidden), owners, cap)
    hid_x = exchange(1, hid_s, hid_r)

    times_ref[...] = key_counts(om_ref, bl_ref, owners, cap, me)
    for name in ("g2", "win2", "wout2"):
        loads[name].wait()
    gain = g2_ref[...]
    finish(hid_x)
    rows32 = join_rows(hid_r, owners, cap).astype(F32)
    center, rstd = norm_stats(rows32)
    normed = (center * rstd * gain).astype(BF16)
    packed = dot(normed, win2_ref[...]).astype(BF16)
    mixed = []
    for t in range(pairs):
        q, k, v = triple(packed, t, d)
        times = times_ref[...]
        s = jnp.where(times > 0.0, dot_bt(two_heads(q), k) * SCALE, -1e30)
        w = jnp.where(times > 0.0, jnp.exp(s - jnp.max(s, axis=-1, keepdims=True)), 0.0)
        p = w / jnp.sum(w * times, axis=-1, keepdims=True)
        p2_ref[t] = p
        pm = (p.astype(BF16).astype(F32) * times).astype(BF16)
        mixed.append(join_heads(dot(pm, v)).astype(BF16))
    mixed = jnp.concatenate(mixed, axis=1)
    split_rows(res_s, dot(mixed, wout2_ref[...]), owners, cap)
    res_x = exchange(2, res_s, res_r)

    a, b, y_, c_, d_ = {}, {}, {}, {}, {}

    def begin(k, left_t, right):
        block = dot(left_t, right).astype(BF16)
        for part in range(replicas):
            grad_ref[k, part // xs_n, part % xs_n] = block[:, part * width : (part + 1) * width]
        a[k] = remote(grad_ref.at[k, 1 - core], ra.at[k], as_.at[k], ar.at[k],
                      (x_me * 2 + 1 - core, me))

    def after_a(k):
        a[k].wait()
        for i in range(xs_n):
            sa[k, i] = (grad_ref[k, core, i].astype(F32) + ra[k, i].astype(F32)).astype(BF16)
        b[k] = []
        for o in range(1, xs_n):
            to = lax.rem(x_me + o, xs_n)
            b[k].append(remote(sa.at[k, to], rb.at[k, o - 1], bs.at[k, o - 1], br.at[k, o - 1],
                               (to * 2 + core, me)))

    def after_b(k):
        finish(b[k])
        total = sa[k, x_me].astype(F32)
        for o in range(1, xs_n):
            total = total + rb[k, o - 1].astype(F32)
        total = total.astype(BF16)
        for e in range(owners):
            sb[k, e % 2, e // 2] = total[e * depth : (e + 1) * depth]
        y_[k] = remote(sb.at[k, 1 - y_me], ry.at[k], ys.at[k], yr.at[k], (dp, z_me * 2 + 1 - y_me))

    def after_y(k):
        y_[k].wait()
        for z in range(zs_n):
            sy[k, z] = (sb[k, y_me, z].astype(F32) + ry[k, z].astype(F32)).astype(BF16)
        c_[k] = []
        for o in range(1, zs_n):
            to = lax.rem(z_me + o, zs_n)
            c_[k].append(remote(sy.at[k, to], rc.at[k, o - 1], cs.at[k, o - 1], cr.at[k, o - 1],
                                (dp, to * 2 + y_me)))

    def after_c(k):
        finish(c_[k])
        total = sy[k, z_me].astype(F32)
        for o in range(1, zs_n):
            total = total + rc[k, o - 1].astype(F32)
        total = total.astype(BF16)
        sc[k] = total
        part = core * xs_n + x_me
        gat[k, part] = total
        d_[k] = []
        for o in range(1, replicas):
            to = lax.rem(dp + o, replicas)
            d_[k].append(remote(sc.at[k], gat.at[k, part], ds_.at[k, o - 1], dr.at[k, o - 1], (to, me)))

    def after_d(k):
        finish(d_[k])
        for part in range(replicas):
            at = (k * replicas + part) * width
            value = gat[k, part].astype(F32) * factor
            if at < 3 * d:
                gproj_ref[:, at : at + width] = value
            else:
                gout_ref[:, at - 3 * d : at - 3 * d + width] = value

    finish(cot_x)
    cot = join_rows(cot_r, owners, cap)
    span = replicas * width
    mixed_t, normed_t = mixed.T, normed.T
    early = [k for k in range(pieces) if k * span >= 3 * d]
    for k in early:
        begin(k, mixed_t, cot[:, k * span - 3 * d : (k + 1) * span - 3 * d])
    back_mixed = dot_bt(cot, wout2_ref[...]).astype(BF16)
    dq, dk, dv = [], [], []
    for t in range(pairs):
        q, k, v = triple(packed, t, d)
        p, times = p2_ref[t], times_ref[...]
        pm = (p.astype(BF16).astype(F32) * times).astype(BF16)
        dm = two_heads(back_mixed[:, t * BLOCK : (t + 1) * BLOCK])
        d_p = dot_bt(dm, v).astype(BF16).astype(F32)
        pt = p * times
        ds = (pt * (d_p - jnp.sum(pt * d_p, axis=-1, keepdims=True)) * SCALE).astype(BF16)
        dq.append(join_heads(dot(ds, k)).astype(BF16))
        dk.append(dot_at(ds, two_heads(q)).astype(BF16))
        dv.append(dot_at(pm, dm).astype(BF16))
    back_packed = jnp.concatenate(dq + dk + dv, axis=1)
    for k in range(pieces):
        if k in early:
            continue
        if (k + 1) * span <= 3 * d:
            begin(k, normed_t, back_packed[:, k * span : (k + 1) * span])
        else:
            begin_split = jnp.concatenate(
                [dot(normed_t, back_packed[:, k * span :]),
                 dot(mixed_t, cot[:, : (k + 1) * span - 3 * d])], axis=1)
            block = begin_split.astype(BF16)
            for part in range(replicas):
                grad_ref[k, part // xs_n, part % xs_n] = block[:, part * width : (part + 1) * width]
            a[k] = remote(grad_ref.at[k, 1 - core], ra.at[k], as_.at[k], ar.at[k],
                          (x_me * 2 + 1 - core, me))
    order = early + [k for k in range(pieces) if k not in early]
    for k in early:
        after_a(k)
    split_rows(bck_s, norm_back(rows32, gain, dot_bt(back_packed, win2_ref[...])), owners, cap)
    bck_x = exchange(3, bck_s, bck_r)
    for k in order:
        if k not in early:
            after_a(k)

    steps = [after_b, after_y, after_c, after_d]
    waves = [
        (step, order[w - n]) for w in range(len(order) + len(steps) - 1)
        for n, step in reversed(list(enumerate(steps))) if 0 <= w - n < len(order)]
    for step, k in waves[:6]:
        step(k)

    finish(res_x)
    finish(bck_x)
    out_ref[0] = (hid_ref[...].astype(F32) + dot_at(place, join_rows(res_r, owners, cap))).astype(BF16)
    grad_hidden = (ct_ref[0].astype(F32) + dot_at(place, join_rows(bck_r, owners, cap))).astype(BF16)
    d_mixed = dot_bt(grad_hidden, wout1_ref[...]).astype(BF16)
    dq, dk, dv = [], [], []
    for t in range(pairs):
        q, k, v = triple(packed_ref, t, d)
        p = probs_ref[t]
        dm = two_heads(d_mixed[:, t * BLOCK : (t + 1) * BLOCK])
        d_p = dot_bt(dm, v).astype(BF16).astype(F32)
        ds = (p * (d_p - jnp.sum(p * d_p, axis=-1, keepdims=True)) * SCALE).astype(BF16)
        dq.append(join_heads(dot(ds, k)).astype(BF16))
        dk.append(dot_at(ds, two_heads(q)).astype(BF16))
        dv.append(dot_at(p.astype(BF16), dm).astype(BF16))
    d_packed = jnp.concatenate(dq + dk + dv, axis=1)
    d_normed = dot_bt(d_packed, win1_ref[...]).astype(BF16).astype(F32)
    dx = norm_back(x_ref[0].astype(F32), g1_ref[...], d_normed).astype(BF16)
    gx_ref[0] = (grad_hidden.astype(F32) + dx.astype(F32)).astype(BF16)

    for step, k in waves[6:]:
        step(k)


def on_device(events, cotangent, intra_gain, intra_proj, intra_out, cross_norm_gain,
              cross_input_weight, cross_output_weight, owner_map, block_lists):
    _, local_rows, d = events.shape
    owners = lax.axis_size("ev")
    replicas = lax.axis_size("dp")
    cap = 2 * local_rows // owners
    total = owners * cap
    pieces = min(4, 4 * d // replicas // 128)
    width = 4 * d // replicas // pieces
    depth = d // owners
    half, zs = replicas // 2, owners // 2
    few = max(half - 1, 1)
    factor = (replicas * owners * local_rows) ** (-0.5)
    gain1 = intra_gain.reshape(1, d)
    gain2 = cross_norm_gain.reshape(1, d)
    dma = pltpu.SemaphoreType.DMA
    ins = [events, cotangent, owner_map, gain1, intra_proj, intra_out,
           gain2, cross_input_weight, cross_output_weight, block_lists]
    scratch = [pltpu.VMEM(a.shape, a.dtype) for a in ins[:9]] + [
        pltpu.VMEM((local_rows, 3 * d), BF16),
        pltpu.VMEM((d // BLOCK, 2 * BLOCK, BLOCK), F32),
        pltpu.VMEM((local_rows, d), BF16),
        pltpu.VMEM((2 * total, total), F32),
        pltpu.VMEM((d // BLOCK, 2 * total, total), F32),
        pltpu.VMEM((pieces, 2, half, d, width), BF16),
    ] + [pltpu.VMEM((owners, cap, d), BF16)] * 8 + [
        pltpu.VMEM((pieces, half, d, width), BF16),
        pltpu.VMEM((pieces, half, d, width), BF16),
        pltpu.VMEM((pieces, few, d, width), BF16),
        pltpu.VMEM((pieces, 2, zs, depth, width), BF16),
        pltpu.VMEM((pieces, zs, depth, width), BF16),
        pltpu.VMEM((pieces, zs, depth, width), BF16),
        pltpu.VMEM((pieces, zs - 1, depth, width), BF16),
        pltpu.VMEM((pieces, depth, width), BF16),
        pltpu.VMEM((pieces, replicas, depth, width), BF16),
        dma((9,)), dma((4, owners)), dma((4, owners)),
        dma((pieces,)), dma((pieces,)),
        dma((pieces, few)), dma((pieces, few)),
        dma((pieces,)), dma((pieces,)),
        dma((pieces, zs - 1)), dma((pieces, zs - 1)),
        dma((pieces, replicas - 1)), dma((pieces, replicas - 1)),
    ]
    vm = pl.BlockSpec(memory_space=pltpu.VMEM)
    outs = [((1, local_rows, d), BF16), ((1, local_rows, d), BF16),
            ((depth, 3 * d), F32), ((depth, d), F32)]
    return tuple(pl.pallas_call(
        functools.partial(fused, owners, cap, (pieces, replicas, width), factor),
        out_shape=[jax.ShapeDtypeStruct(s, t) for s, t in outs],
        in_specs=[pl.BlockSpec(memory_space=pltpu.HBM)] * 9 + [pl.BlockSpec(memory_space=pltpu.SMEM)],
        out_specs=[vm] * 4,
        scratch_shapes=scratch,
        compiler_params=pltpu.CompilerParams(
            vmem_limit_bytes=VMEM_LIMIT, collective_id=0, has_side_effects=True),
    )(*ins))


def solution(mesh):
    row = P("dp", "ev", None)
    return jax.shard_map(
        on_device,
        mesh=mesh,
        in_specs=(row, row, P(), P(), P(), P(), P(), P(), P("dp", None), P("dp", "ev", None, None)),
        out_specs=(row, row, P("ev", None), P("ev", None)),
        check_vma=False,
    )
```
